32 devices in a mesh: gx: 4 (over x, core), gy: 8 (over z, y).
Axes of the slice: x: 2, y: 2, z: 4, core: 2. Of those that a mesh axis runs over, the one named last changes fastest.
Arguments:
- state: float32 [8, 16, 96, 2048], P(None, None, 'gy', 'gx'), may hold values from -6 to 6
- register: float32 [8, 16, 96, 2048], P(None, None, 'gy', 'gx'), may hold values from -6 to 6
- checkpoint: bfloat16 [8, 16, 96, 2048], P(None, None, 'gy', 'gx'), may hold values from -6 to 6
- velocity: float32 [3, 16, 96, 2048], P(None, None, 'gy', 'gx'), may hold values from -4 to 4
- diffusivity: float32 [16, 96, 2048], P(None, 'gy', 'gx'), may hold values from 0.02 to 0.3
Outputs:
- new_state: float32 [8, 16, 96, 2048], P(None, None, 'gy', 'gx')
- new_register: float32 [8, 16, 96, 2048], P(None, None, 'gy', 'gx')
- gram: float32 [2048, 2048], P('gx', 'gy')
The draws below stay inside these ranges and needn't reach their ends.
All inputs are finite; a program needn't handle non-finite values.
Results may differ from the reference program's by a relative error of at most 0.0003.
Values sent between devices are 32-bit elements; how exact they have to be, the bound alone decides.
A program may use at most 64 MiB of HBM per device.

```python
import math
import jax
import jax.numpy as jnp
from jax import lax

NX = 2048
NV = 8
NZ = 16
NY = 96


def shard_levels(stream_key, dims, cuts, smallest, high):
    factor_of, own = 1.0, jax.random.fold_in(stream_key, 6)
    for dim, shards_of in cuts:
        steps = jnp.exp(jax.random.uniform(jax.random.fold_in(own, dim), (shards_of,), jnp.float32, smallest / len(cuts), high / len(cuts)))
        factor_of = factor_of * jnp.repeat(steps, dims[dim] // shards_of).reshape([-1 if axis == dim else 1 for axis in range(len(dims))])
    return factor_of


def centred(rng, dims, scale, most, shards=(), held_as=jnp.bfloat16):
    entries = jax.random.normal(rng, dims, jnp.float32) * scale
    if len(shards) > 0:
        entries = shard_levels(rng, dims, shards, -0.22, 0.18) * entries
    return jnp.clip(entries, min=-most, max=most).astype(held_as)


def setup_inputs(seed: int = 0) -> dict:
    seeds = jax.random.split(jax.random.key(seed), 6)
    state = centred(seeds[0], (NV, NZ, NY, NX), 1.0, 6.0, ((2, 8), (3, 4)), jnp.float32)
    register = centred(seeds[1], (NV, NZ, NY, NX), 1.0, 6.0, ((2, 8), (3, 4)), jnp.float32)
    checkpoint = centred(seeds[2], (NV, NZ, NY, NX), 1.0, 6.0, ((2, 8), (3, 4)))
    velocity = centred(seeds[3], (3, NZ, NY, NX), 1.0, 4.0, ((2, 8), (3, 4)), jnp.float32)
    diffusivity = jnp.clip(jnp.exp(math.log(0.3) - 2.7080503 * jax.random.uniform(seeds[4], (NZ, NY, NX), jnp.float32) ** shard_levels(seeds[4], (NZ, NY, NX), ((1, 8), (2, 4)), -0.2, 0.2)), 0.02, 0.3)
    return {"state": state, "register": register, "checkpoint": checkpoint, "velocity": velocity, "diffusivity": diffusivity}


step_size = 0.3
carry_weight = -5.0 / 9.0
update_weight = 15.0 / 16.0


def first_diff(field, axis):
    plus_one = jnp.roll(field, -1, axis)
    minus_one = jnp.roll(field, 1, axis)
    plus_two = jnp.roll(field, -2, axis)
    minus_two = jnp.roll(field, 2, axis)
    return (8.0 * (plus_one - minus_one) - (plus_two - minus_two)) / 12.0


def second_diff(field, axis):
    plus_one = jnp.roll(field, -1, axis)
    minus_one = jnp.roll(field, 1, axis)
    plus_two = jnp.roll(field, -2, axis)
    minus_two = jnp.roll(field, 2, axis)
    return (16.0 * (plus_one + minus_one) - (plus_two + minus_two) - 30.0 * field) / 12.0


def reference(state, register, checkpoint, velocity, diffusivity):
    advect = velocity[0][None] * first_diff(state, 3) + velocity[1][None] * first_diff(state, 2) + velocity[2][None] * first_diff(state, 1)
    spread = second_diff(state, 3) + second_diff(state, 2) + second_diff(state, 1)
    tendency = -advect + diffusivity[None] * spread
    new_register = carry_weight * register + step_size * tendency
    new_state = state + update_weight * new_register
    change = new_state - checkpoint.astype(jnp.float32)
    columns = NV * NZ * NY
    unfolded = jnp.moveaxis(change, 3, 0).reshape(NX, columns)
    gram = jnp.dot(unfolded, unfolded.T, preferred_element_type=jnp.float32, precision=lax.Precision.HIGHEST)
    gram = gram / jnp.float32(columns)
    return new_state, new_register, gram
```

```python
import functools

import jax
import jax.numpy as jnp
from jax import lax
from jax.experimental import pallas as pl
from jax.experimental.pallas import tpu as pltpu
from jax.sharding import PartitionSpec as P

step_size = 0.3
carry_weight = -5.0 / 9.0
update_weight = 15.0 / 16.0
LANES = 128
PACK = LANES // 2
MESH = pl.DeviceIdType.MESH
VMEM = pltpu.VMEM
LIMIT = 56 * 2**20


def halo_kernel(gx, gy, state, y_halo, x_halo, y_send, x_send, y_ssem, y_rsem, x_ssem, x_rsem):
    planes, rows, width = state.shape
    me_x, me_y = lax.axis_index("gx"), lax.axis_index("gy")
    x_up, x_down = lax.rem(me_x + 1, gx), lax.rem(me_x + gx - 1, gx)
    y_up, y_down = lax.rem(me_y + 1, gy), lax.rem(me_y + gy - 1, gy)
    barrier = pltpu.get_barrier_semaphore()
    for device in ((x_up, me_y), (x_down, me_y), (me_x, y_up), (me_x, y_down)):
        pl.semaphore_signal(barrier, inc=1, device_id=device, device_id_type=MESH)

    def pack_y(group, _):
        for k in range(4):
            y_send[0, group, 2 * k : 2 * k + 2, :] = state[4 * group + k, 0:2, :]
            y_send[1, group, 2 * k : 2 * k + 2, :] = state[4 * group + k, rows - 2 : rows, :]
        return 0

    lax.fori_loop(0, planes // 4, pack_y, 0)
    pl.semaphore_wait(barrier, 4)
    copies = []
    for side, target in ((0, y_down), (1, y_up)):
        copies.append(
            pltpu.make_async_remote_copy(
                src_ref=y_send.at[side],
                dst_ref=y_halo.at[side],
                send_sem=y_ssem.at[side],
                recv_sem=y_rsem.at[side],
                device_id=(me_x, target),
                device_id_type=MESH,
            )
        )
        copies[-1].start()

    lane = lax.broadcasted_iota(jnp.int32, (rows, LANES), 1) // 2
    for group in range(planes // PACK):

        def pack_x(pos, kept):
            low, high = kept
            plane = group * PACK + pos
            first = pltpu.roll(state[plane, :, 0:LANES], 2 * pos, 1)
            last = pltpu.roll(state[plane, :, width - LANES : width], lax.rem(2 * pos + 2, LANES), 1)
            return (jnp.where(lane == pos, first, low), jnp.where(lane == pos, last, high))

        zero = jnp.zeros((rows, LANES), jnp.float32)
        low, high = lax.fori_loop(0, PACK, pack_x, (zero, zero))
        x_send[0, group, 0:rows, :] = low
        x_send[1, group, 0:rows, :] = high
        x_send[0, group, rows:, :] = jnp.zeros((x_send.shape[2] - rows, LANES), jnp.float32)
        x_send[1, group, rows:, :] = jnp.zeros((x_send.shape[2] - rows, LANES), jnp.float32)
    for side, target in ((0, x_down), (1, x_up)):
        copies.append(
            pltpu.make_async_remote_copy(
                src_ref=x_send.at[side],
                dst_ref=x_halo.at[side],
                send_sem=x_ssem.at[side],
                recv_sem=x_rsem.at[side],
                device_id=(target, me_y),
                device_id_type=MESH,
            )
        )
        copies[-1].start()
    for copy in copies:
        copy.wait()


def halos(state, gx, gy):
    planes, rows, width = state.shape
    tall = -(-rows // 8) * 8
    y_shape, x_shape = (2, planes // 4, 8, width), (2, planes // PACK, tall, LANES)
    return pl.pallas_call(
        functools.partial(halo_kernel, gx, gy),
        out_shape=(jax.ShapeDtypeStruct(y_shape, jnp.float32), jax.ShapeDtypeStruct(x_shape, jnp.float32)),
        in_specs=[pl.BlockSpec(memory_space=VMEM)],
        out_specs=[pl.BlockSpec(memory_space=VMEM)] * 2,
        scratch_shapes=[VMEM(y_shape, jnp.float32), VMEM(x_shape, jnp.float32)] + [pltpu.SemaphoreType.DMA((2,))] * 4,
        compiler_params=pltpu.CompilerParams(collective_id=0, has_side_effects=True, vmem_limit_bytes=LIMIT),
    )(state)


def stencil_kernel(state, register, checkpoint, velocity, diffusivity, y_halo, x_halo, new_state, new_register, change, ext):
    nz, rows, width = state.shape
    pos0 = lax.rem(pl.program_id(0), PACK // nz) * nz
    tall = rows + 4
    whole = width + LANES
    lane = lax.broadcasted_iota(jnp.int32, (x_halo.shape[2], LANES), 1)
    for z in range(nz):
        ext[z, 0:rows, :] = state[z]
        part = 2 * (z % 4)
        ext[z, rows : rows + 2, :] = y_halo[0, z // 4, part : part + 2, :]
        ext[z, rows + 2 : tall, :] = y_halo[1, z // 4, part : part + 2, :]
    for z in range(nz):
        center = state[z]
        high = ext[z]
        pos = pos0 + z
        right = pltpu.roll(x_halo[0, 0], lax.rem(LANES - 2 * pos, LANES), 1)
        left = pltpu.roll(x_halo[1, 0], lax.rem(2 * LANES - 2 - 2 * pos, LANES), 1)
        beside = jnp.where(lane < 2, right, left)[:rows]
        wide = jnp.concatenate([center, beside], axis=1)
        near = []
        far = []
        advect = None
        for d in range(3):
            if d == 0:
                p1, m1, p2, m2 = (pltpu.roll(wide, k, 1)[:, :width] for k in (whole - 1, 1, whole - 2, 2))
            elif d == 1:
                p1, m1, p2, m2 = (pltpu.roll(high, k, 0)[:rows] for k in (tall - 1, 1, tall - 2, 2))
            else:
                p1, m1, p2, m2 = (state[(z + k) % nz] for k in (1, -1, 2, -2))
            term = velocity[d, z] * (8.0 * (p1 - m1) - (p2 - m2))
            advect = term if advect is None else advect + term
            near.append(p1 + m1)
            far.append(p2 + m2)
        spread = 16.0 * (near[0] + near[1] + near[2]) - (far[0] + far[1] + far[2]) - 90.0 * center
        tendency = (diffusivity[z] * spread - advect) * (1.0 / 12.0)
        increment = carry_weight * register[z] + step_size * tendency
        updated = center + update_weight * increment
        new_register[z] = increment
        new_state[z] = updated
        moved = updated - checkpoint[z].astype(jnp.float32)
        for q in range(width // LANES):
            change[q, rows * z : rows * z + rows, :] = moved[:, q * LANES : (q + 1) * LANES]


def stencil(state, register, checkpoint, velocity, diffusivity, y_halo, x_halo):
    planes, rows, width = state.shape
    nz = diffusivity.shape[0]
    nv = planes // nz
    per_group = PACK // nz
    field = pl.BlockSpec((nz, rows, width), lambda v: (v, 0, 0))
    tall = x_halo.shape[2]
    return pl.pallas_call(
        stencil_kernel,
        grid=(nv,),
        out_shape=(
            jax.ShapeDtypeStruct(state.shape, jnp.float32),
            jax.ShapeDtypeStruct(state.shape, jnp.float32),
            jax.ShapeDtypeStruct((width // LANES, planes * rows, LANES), jnp.float32),
        ),
        in_specs=[
            field,
            field,
            field,
            pl.BlockSpec((3, nz, rows, width), lambda v: (0, 0, 0, 0)),
            pl.BlockSpec((nz, rows, width), lambda v: (0, 0, 0)),
            pl.BlockSpec((2, nz // 4, 8, width), lambda v: (0, v, 0, 0)),
            pl.BlockSpec((2, 1, tall, LANES), lambda v: (0, v // per_group, 0, 0)),
        ],
        out_specs=[field, field, pl.BlockSpec((width // LANES, nz * rows, LANES), lambda v: (0, v, 0))],
        scratch_shapes=[VMEM((nz, rows + 4, width), jnp.float32)],
        compiler_params=pltpu.CompilerParams(vmem_limit_bytes=LIMIT),
        cost_estimate=pl.CostEstimate(flops=50 * planes * rows * width, bytes_accessed=28 * planes * rows * width, transcendentals=0),
    )(state, register, checkpoint, velocity, diffusivity, y_halo, x_halo)


def split(value):
    high = value.astype(jnp.bfloat16)
    return high, (value - high.astype(jnp.float32)).astype(jnp.bfloat16)


def gram_kernel(
    total, own, out, held, lhs_high, lhs_low, product, y_out, y_in, kept, z_in,
    core_ssem, core_rsem, x_ssem, x_rsem, pass_ssem, pass_rsem, y_ssem, y_rsem, z_ssem, z_rsem,
):
    chunks, depth, _ = own.shape
    parts = chunks // 2
    width = chunks * LANES
    i, j = lax.axis_index("gx"), lax.axis_index("gy")
    i0, i1 = lax.rem(i, 2), i // 2
    y, z = lax.rem(j, 2), j // 2
    core = (2 * i1 + 1 - i0, j)
    across = (2 * (1 - i1) + i0, j)
    y_partner = (i, 2 * z + 1 - y)
    blocks = [2 * lax.rem(i1 + s // 2, 2) + lax.rem(i0 + s % 2, 2) for s in range(4)]
    barrier = pltpu.get_barrier_semaphore()
    for device in (core, across, y_partner, *((i, 2 * lax.rem(z + k, 4) + y) for k in (1, 2, 3))):
        pl.semaphore_signal(barrier, inc=1, device_id=device, device_id_type=MESH)
    pl.semaphore_wait(barrier, 6)

    def remote(src, dst, send, recv, device):
        return pltpu.make_async_remote_copy(
            src_ref=src, dst_ref=dst, send_sem=send, recv_sem=recv, device_id=device, device_id_type=MESH
        )

    def chunk_of(t):
        return lax.rem(t // parts + 1 + y, 2) * parts + lax.rem(t, parts)

    def x_copy(t):
        q = chunk_of(t)
        return remote(own.at[q], held.at[1, q], x_ssem.at[t], x_rsem.at[t], across)

    def pass_copy(t):
        q = chunk_of(t)
        return remote(held.at[1, q], held.at[2, q], pass_ssem.at[t], pass_rsem.at[t], core)

    def y_copy(s, part):
        return remote(y_out.at[s, part], y_in.at[s, part], y_ssem.at[s, part], y_rsem.at[s, part], y_partner)

    def z_copy(s, part):
        back = lax.rem(z - blocks[s] + 4, 4)
        slot = jnp.maximum(back, 1) - 1
        return remote(
            kept.at[s, part], z_in.at[slot, part], z_ssem.at[s, part], z_rsem.at[slot, part], (i, 2 * blocks[s] + y)
        )

    for t in range(chunks):
        x_copy(t).start()
    to_core = remote(own, held.at[0], core_ssem, core_rsem, core)
    to_core.start()

    def turn(q, _):
        high, low = split(own[q].T)
        rows = pl.ds(pl.multiple_of(q * LANES, LANES), LANES)
        lhs_high[rows, :] = high
        lhs_low[rows, :] = low
        return 0

    lax.fori_loop(0, chunks, turn, 0)

    step = depth // 3 if depth % (3 * LANES) == 0 else depth

    def multiply(left, right):
        for k in range(0, depth, step):
            block = jnp.concatenate([left[k : k + step, :], right[k : k + step, :]], axis=1)
            high, low = split(block)
            mine_high, mine_low = lhs_high[:, k : k + step], lhs_low[:, k : k + step]
            dot = functools.partial(jnp.dot, preferred_element_type=jnp.float32)
            term = dot(mine_high, high) + dot(mine_high, low) + dot(mine_low, high)
            if k == 0:
                product[...] = term
            else:
                product[...] += term

    def chunk_pair(base, t, left, right):
        multiply(left, right)
        part = lax.rem(t, parts)

        @pl.when(t < parts)
        def _():
            for s in range(2):
                y_out[base + s, part] = product[:, s * LANES : (s + 1) * LANES]
                y_copy(base + s, part).start()

        @pl.when(t >= parts)
        def _():
            for s in range(2):
                kept[base + s, part] = product[:, s * LANES : (s + 1) * LANES]

    def forward(base, part):
        for s in (base, base + 1):
            y_copy(s, part).wait_recv()
            kept[s, part] += y_in[s, part]

            @pl.when(blocks[s] != z)
            def _():
                z_copy(s, part).start()

    to_core.wait_recv()

    def near(t, _):
        q = chunk_of(t)
        chunk_pair(0, t, own.at[q], held.at[0, q])
        return 0

    lax.fori_loop(0, chunks, near, 0)

    def far(t, _):
        q = chunk_of(t)
        x_copy(t).wait_recv()
        pass_copy(t).start()

        @pl.when(t == parts)
        def _():
            for part in range(parts):
                forward(0, part)

        pass_copy(t).wait_recv()
        chunk_pair(2, t, held.at[1, q], held.at[2, q])

        @pl.when(t >= parts)
        def _():
            forward(2, t - parts)

        return 0

    lax.fori_loop(0, chunks, far, 0)
    for s in range(4):

        @pl.when(blocks[s] == z)
        def _():
            for part in range(parts):
                out[:, part * LANES : (part + 1) * LANES] = kept[s, part]

    for part in range(parts):
        for slot in range(3):
            remote(kept.at[0, part], z_in.at[slot, part], z_ssem.at[0, part], z_rsem.at[slot, part], core).wait_recv()
        cols = slice(part * LANES, (part + 1) * LANES)
        out[:, cols] = (out[:, cols] + z_in[0, part] + (z_in[1, part] + z_in[2, part])) / jnp.float32(total)
    to_core.wait_send()
    for t in range(chunks):
        x_copy(t).wait_send()
        pass_copy(t).wait_send()
    for s in range(4):
        for part in range(parts):
            y_copy(s, part).wait_send()

            @pl.when(blocks[s] != z)
            def _():
                z_copy(s, part).wait_send()


def gram_blocks(change, total):
    chunks, depth, _ = change.shape
    width = chunks * LANES
    parts = chunks // 2
    tile = (4, parts, width, LANES)
    dma = pltpu.SemaphoreType.DMA
    return pl.pallas_call(
        functools.partial(gram_kernel, total),
        out_shape=jax.ShapeDtypeStruct((width, parts * LANES), jnp.float32),
        in_specs=[pl.BlockSpec(memory_space=VMEM)],
        out_specs=pl.BlockSpec(memory_space=VMEM),
        scratch_shapes=[
            VMEM((3, chunks, depth, LANES), jnp.float32),
            VMEM((width, depth), jnp.bfloat16),
            VMEM((width, depth), jnp.bfloat16),
            VMEM((width, 2 * LANES), jnp.float32),
            VMEM(tile, jnp.float32),
            VMEM(tile, jnp.float32),
            VMEM(tile, jnp.float32),
            VMEM((3, parts, width, LANES), jnp.float32),
            dma, dma,
            dma((chunks,)), dma((chunks,)),
            dma((chunks,)), dma((chunks,)),
            dma((4, parts)), dma((4, parts)),
            dma((4, parts)), dma((3, parts)),
        ],
        compiler_params=pltpu.CompilerParams(collective_id=1, has_side_effects=True, vmem_limit_bytes=LIMIT),
    )(change)


def on_device(state, register, checkpoint, velocity, diffusivity):
    gx, gy = lax.axis_size("gx"), lax.axis_size("gy")
    nv, nz, rows, width = state.shape
    flat = (nv * nz, rows, width)
    planes = state.reshape(flat)
    y_halo, x_halo = halos(planes, gx, gy)
    new_state, new_register, change = stencil(
        planes, register.reshape(flat), checkpoint.reshape(flat), velocity, diffusivity, y_halo, x_halo
    )
    total = nv * nz * rows * gy
    if gx == 4 and gy == 2 * gx and width % (2 * LANES) == 0:
        gram = gram_blocks(change, total)
    else:
        mine = jnp.moveaxis(change, 0, 1).reshape(nv * nz * rows, width)
        block_rows = lax.dot_general(
            mine,
            lax.all_gather(mine, "gx", axis=1, tiled=True),
            (((0,), (0,)), ((), ())),
            preferred_element_type=jnp.float32,
            precision=lax.Precision.HIGHEST,
        )
        gram = lax.psum_scatter(block_rows, "gy", scatter_dimension=1, tiled=True) / jnp.float32(total)
    return (new_state.reshape(state.shape), new_register.reshape(state.shape), gram)


def solution(mesh):
    tiles = P(None, None, "gy", "gx")
    in_specs = (tiles, tiles, tiles, tiles, P(None, "gy", "gx"))
    out_specs = (tiles, tiles, P("gx", "gy"))
    return jax.shard_map(on_device, mesh=mesh, in_specs=in_specs, out_specs=out_specs, check_vma=False)
```

```python
import functools

import jax
import jax.numpy as jnp
from jax import lax
from jax.experimental import pallas as pl
from jax.experimental.pallas import tpu as pltpu
from jax.sharding import PartitionSpec as P

step_size = 0.3
carry_weight = -5.0 / 9.0
update_weight = 15.0 / 16.0
LANES = 128
MESH = pl.DeviceIdType.MESH
VMEM = pltpu.VMEM
LIMIT = 56 * 2**20


def pack_columns(state, v, x_send):
    _, rows, nz, width = state.shape
    lane = lax.broadcasted_iota(jnp.int32, (nz, LANES), 1) // 2
    low = jnp.zeros((nz, LANES), jnp.float32)
    high = low
    for y in range(rows):
        first = state[v, y, :, 0:LANES]
        last = pltpu.roll(state[v, y, :, width - LANES : width], (2 * y + 2) % LANES, 1)
        low = jnp.where(lane == y, pltpu.roll(first, 2 * y, 1) if y else first, low)
        high = jnp.where(lane == y, last, high)
    x_send[0, v] = low
    x_send[1, v] = high


def beside_columns(from_right, from_left, y):
    lane = lax.broadcasted_iota(jnp.int32, from_right.shape, 1)
    right = pltpu.roll(from_right, LANES - 2 * y, 1) if y else from_right
    left = pltpu.roll(from_left, (2 * LANES - 2 - 2 * y) % LANES, 1)
    return jnp.where(lane < 2, right, left)


def halo_copies(gx, gy, state, y_halo, x_send, x_halo, y_ssem, y_rsem, x_ssem, x_rsem):
    rows = state.shape[1]
    me_x, me_y = lax.axis_index("gx"), lax.axis_index("gy")
    x_up, x_down = lax.rem(me_x + 1, gx), lax.rem(me_x + gx - 1, gx)
    y_up, y_down = lax.rem(me_y + 1, gy), lax.rem(me_y + gy - 1, gy)
    along_x, along_y = [], []
    for side, target, at in ((0, y_down, 0), (1, y_up, rows - 2)):
        along_y.append(
            pltpu.make_async_remote_copy(
                src_ref=state.at[:, at : at + 2],
                dst_ref=y_halo.at[side],
                send_sem=y_ssem.at[side],
                recv_sem=y_rsem.at[side],
                device_id=(me_x, target),
                device_id_type=MESH,
            )
        )
    for side, target in ((0, x_down), (1, x_up)):
        along_x.append(
            pltpu.make_async_remote_copy(
                src_ref=x_send.at[side],
                dst_ref=x_halo.at[side],
                send_sem=x_ssem.at[side],
                recv_sem=x_rsem.at[side],
                device_id=(target, me_y),
                device_id_type=MESH,
            )
        )
    return along_x, along_y, ((x_up, me_y), (x_down, me_y), (me_x, y_up), (me_x, y_down))


def halo_kernel(gx, gy, state, y_halo, x_halo, x_send, y_ssem, y_rsem, x_ssem, x_rsem):
    along_x, along_y, near = halo_copies(gx, gy, state, y_halo, x_send, x_halo, y_ssem, y_rsem, x_ssem, x_rsem)
    barrier = pltpu.get_barrier_semaphore()
    for device in near:
        pl.semaphore_signal(barrier, inc=1, device_id=device, device_id_type=MESH)
    for v in range(state.shape[0]):
        pack_columns(state, v, x_send)
    pl.semaphore_wait(barrier, 4)
    for copy in along_x + along_y:
        copy.start()
    for copy in along_x + along_y:
        copy.wait()


def halos(state, gx, gy):
    nv, _, nz, width = state.shape
    y_shape, x_shape = (2, nv, 2, nz, width), (2, nv, nz, LANES)
    return pl.pallas_call(
        functools.partial(halo_kernel, gx, gy),
        out_shape=(jax.ShapeDtypeStruct(y_shape, jnp.float32), jax.ShapeDtypeStruct(x_shape, jnp.float32)),
        in_specs=[pl.BlockSpec(memory_space=VMEM)],
        out_specs=[pl.BlockSpec(memory_space=VMEM)] * 2,
        scratch_shapes=[VMEM(x_shape, jnp.float32)] + [pltpu.SemaphoreType.DMA((2,))] * 4,
        compiler_params=pltpu.CompilerParams(collective_id=0, has_side_effects=True, vmem_limit_bytes=LIMIT),
    )(state)


def advance(center, beside, around, register, checkpoint, speeds, spreading):
    nz, width = center.shape
    whole = width + LANES
    wide = jnp.concatenate([center, beside], axis=1)
    along_x = [pltpu.roll(wide, k, 1)[:, :width] for k in (whole - 1, 1, whole - 2, 2)]
    along_z = [pltpu.roll(center, k, 0) for k in (nz - 1, 1, nz - 2, 2)]
    advect = near = far = None
    for speed, (p1, m1, p2, m2) in zip(speeds, (along_x, around, along_z)):
        term = speed * (8.0 * (p1 - m1) - (p2 - m2))
        advect = term if advect is None else advect + term
        near = p1 + m1 if near is None else near + (p1 + m1)
        far = p2 + m2 if far is None else far + (p2 + m2)
    spread = 16.0 * near - far - 90.0 * center
    tendency = (spreading * spread - advect) * (1.0 / 12.0)
    increment = carry_weight * register + step_size * tendency
    updated = center + update_weight * increment
    return updated, increment, updated - checkpoint.astype(jnp.float32)


def stencil_kernel(state, register, checkpoint, velocity, diffusivity, y_halo, x_halo, new_state, new_register, change):
    _, rows, nz, width = state.shape

    def plane(y):
        if y < 0:
            return y_halo[1, 0, y + 2]
        return y_halo[0, 0, y - rows] if y >= rows else state[0, y]

    for y in range(rows):
        updated, increment, moved = advance(
            plane(y),
            beside_columns(x_halo[0, 0], x_halo[1, 0], y),
            [plane(y + k) for k in (1, -1, 2, -2)],
            register[0, y],
            checkpoint[0, y],
            [velocity[d, y] for d in range(3)],
            diffusivity[y],
        )
        new_register[0, y] = increment
        new_state[0, y] = updated
        for q in range(width // LANES):
            change[q, nz * y : nz * y + nz, :] = moved[:, q * LANES : (q + 1) * LANES]


def stencil(state, register, checkpoint, velocity, diffusivity, y_halo, x_halo):
    nv, rows, nz, width = state.shape
    cells = nv * rows * nz * width
    field = pl.BlockSpec((1, rows, nz, width), lambda v: (v, 0, 0, 0))
    return pl.pallas_call(
        stencil_kernel,
        grid=(nv,),
        out_shape=(
            jax.ShapeDtypeStruct(state.shape, jnp.float32),
            jax.ShapeDtypeStruct(state.shape, jnp.float32),
            jax.ShapeDtypeStruct((width // LANES, nv * rows * nz, LANES), jnp.float32),
        ),
        in_specs=[
            field,
            field,
            field,
            pl.BlockSpec((3, rows, nz, width), lambda v: (0, 0, 0, 0)),
            pl.BlockSpec((rows, nz, width), lambda v: (0, 0, 0)),
            pl.BlockSpec((2, 1, 2, nz, width), lambda v: (0, v, 0, 0, 0)),
            pl.BlockSpec((2, 1, nz, LANES), lambda v: (0, v, 0, 0)),
        ],
        out_specs=[field, field, pl.BlockSpec((width // LANES, rows * nz, LANES), lambda v: (0, v, 0))],
        compiler_params=pltpu.CompilerParams(vmem_limit_bytes=LIMIT),
        cost_estimate=pl.CostEstimate(flops=50 * cells, bytes_accessed=28 * cells, transcendentals=0),
    )(state, register, checkpoint, velocity, diffusivity, y_halo, x_halo)


def split(value):
    high = value.astype(jnp.bfloat16)
    return high, (value - high.astype(jnp.float32)).astype(jnp.bfloat16)


def gram_kernel(
    total, own, out, held, lhs_high, lhs_low, product, y_out, y_in, kept, z_in,
    core_ssem, core_rsem, x_ssem, x_rsem, pass_ssem, pass_rsem, y_ssem, y_rsem, z_ssem, z_rsem,
):
    chunks, depth, _ = own.shape
    parts = chunks // 2
    width = chunks * LANES
    i, j = lax.axis_index("gx"), lax.axis_index("gy")
    i0, i1 = lax.rem(i, 2), i // 2
    y, z = lax.rem(j, 2), j // 2
    core = (2 * i1 + 1 - i0, j)
    across = (2 * (1 - i1) + i0, j)
    y_partner = (i, 2 * z + 1 - y)
    blocks = [2 * lax.rem(i1 + s // 2, 2) + lax.rem(i0 + s % 2, 2) for s in range(4)]
    barrier = pltpu.get_barrier_semaphore()
    for device in (core, across, y_partner, *((i, 2 * lax.rem(z + k, 4) + y) for k in (1, 2, 3))):
        pl.semaphore_signal(barrier, inc=1, device_id=device, device_id_type=MESH)
    pl.semaphore_wait(barrier, 6)

    def remote(src, dst, send, recv, device):
        return pltpu.make_async_remote_copy(
            src_ref=src, dst_ref=dst, send_sem=send, recv_sem=recv, device_id=device, device_id_type=MESH
        )

    def chunk_of(t):
        return lax.rem(t // parts + 1 + y, 2) * parts + lax.rem(t, parts)

    def x_copy(t):
        q = chunk_of(t)
        return remote(own.at[q], held.at[1, q], x_ssem.at[t], x_rsem.at[t], across)

    def pass_copy(t):
        q = chunk_of(t)
        return remote(held.at[1, q], held.at[2, q], pass_ssem.at[t], pass_rsem.at[t], core)

    def y_copy(s, part):
        return remote(y_out.at[s, part], y_in.at[s, part], y_ssem.at[s, part], y_rsem.at[s, part], y_partner)

    def z_copy(s, part):
        back = lax.rem(z - blocks[s] + 4, 4)
        slot = jnp.maximum(back, 1) - 1
        return remote(
            kept.at[s, part], z_in.at[slot, part], z_ssem.at[s, part], z_rsem.at[slot, part], (i, 2 * blocks[s] + y)
        )

    for t in range(chunks):
        x_copy(t).start()
    to_core = remote(own, held.at[0], core_ssem, core_rsem, core)
    to_core.start()

    def turn(q, _):
        high, low = split(own[q].T)
        rows = pl.ds(pl.multiple_of(q * LANES, LANES), LANES)
        lhs_high[rows, :] = high
        lhs_low[rows, :] = low
        return 0

    lax.fori_loop(0, chunks, turn, 0)

    step = depth // 3 if depth % (3 * LANES) == 0 else depth

    def multiply(left, right):
        for k in range(0, depth, step):
            block = jnp.concatenate([left[k : k + step, :], right[k : k + step, :]], axis=1)
            high, low = split(block)
            mine_high, mine_low = lhs_high[:, k : k + step], lhs_low[:, k : k + step]
            dot = functools.partial(jnp.dot, preferred_element_type=jnp.float32)
            term = dot(mine_high, high) + dot(mine_high, low) + dot(mine_low, high)
            if k == 0:
                product[...] = term
            else:
                product[...] += term

    def chunk_pair(base, t, left, right):
        multiply(left, right)
        part = lax.rem(t, parts)

        @pl.when(t < parts)
        def _():
            for s in range(2):
                y_out[base + s, part] = product[:, s * LANES : (s + 1) * LANES]
                y_copy(base + s, part).start()

        @pl.when(t >= parts)
        def _():
            for s in range(2):
                kept[base + s, part] = product[:, s * LANES : (s + 1) * LANES]

    def forward(base, part):
        for s in (base, base + 1):
            y_copy(s, part).wait_recv()
            kept[s, part] += y_in[s, part]

            @pl.when(blocks[s] != z)
            def _():
                z_copy(s, part).start()

    to_core.wait_recv()

    def near(t, _):
        q = chunk_of(t)
        chunk_pair(0, t, own.at[q], held.at[0, q])
        return 0

    lax.fori_loop(0, chunks, near, 0)

    def far(t, _):
        q = chunk_of(t)
        x_copy(t).wait_recv()
        pass_copy(t).start()

        @pl.when(t == parts)
        def _():
            for part in range(parts):
                forward(0, part)

        pass_copy(t).wait_recv()
        chunk_pair(2, t, held.at[1, q], held.at[2, q])

        @pl.when(t >= parts)
        def _():
            forward(2, t - parts)

        return 0

    lax.fori_loop(0, chunks, far, 0)
    for s in range(4):

        @pl.when(blocks[s] == z)
        def _():
            for part in range(parts):
                out[:, part * LANES : (part + 1) * LANES] = kept[s, part]

    for part in range(parts):
        for slot in range(3):
            remote(kept.at[0, part], z_in.at[slot, part], z_ssem.at[0, part], z_rsem.at[slot, part], core).wait_recv()
        cols = slice(part * LANES, (part + 1) * LANES)
        out[:, cols] = (out[:, cols] + z_in[0, part] + (z_in[1, part] + z_in[2, part])) / jnp.float32(total)
    to_core.wait_send()
    for t in range(chunks):
        x_copy(t).wait_send()
        pass_copy(t).wait_send()
    for s in range(4):
        for part in range(parts):
            y_copy(s, part).wait_send()

            @pl.when(blocks[s] != z)
            def _():
                z_copy(s, part).wait_send()


def gram_blocks(change, total):
    chunks, depth, _ = change.shape
    width = chunks * LANES
    parts = chunks // 2
    tile = (4, parts, width, LANES)
    dma = pltpu.SemaphoreType.DMA
    return pl.pallas_call(
        functools.partial(gram_kernel, total),
        out_shape=jax.ShapeDtypeStruct((width, parts * LANES), jnp.float32),
        in_specs=[pl.BlockSpec(memory_space=VMEM)],
        out_specs=pl.BlockSpec(memory_space=VMEM),
        scratch_shapes=[
            VMEM((3, chunks, depth, LANES), jnp.float32),
            VMEM((width, depth), jnp.bfloat16),
            VMEM((width, depth), jnp.bfloat16),
            VMEM((width, 2 * LANES), jnp.float32),
            VMEM(tile, jnp.float32),
            VMEM(tile, jnp.float32),
            VMEM(tile, jnp.float32),
            VMEM((3, parts, width, LANES), jnp.float32),
            dma, dma,
            dma((chunks,)), dma((chunks,)),
            dma((chunks,)), dma((chunks,)),
            dma((4, parts)), dma((4, parts)),
            dma((4, parts)), dma((3, parts)),
        ],
        compiler_params=pltpu.CompilerParams(collective_id=1, has_side_effects=True, vmem_limit_bytes=LIMIT),
    )(change)


def on_device(state, register, checkpoint, velocity, diffusivity):
    gx, gy = lax.axis_size("gx"), lax.axis_size("gy")
    nv, nz, rows, width = state.shape
    by_plane = functools.partial(jnp.swapaxes, axis1=1, axis2=2)
    planes = by_plane(state)
    y_halo, x_halo = halos(planes, gx, gy)
    new_state, new_register, change = stencil(
        planes,
        by_plane(register),
        by_plane(checkpoint),
        by_plane(velocity),
        jnp.swapaxes(diffusivity, 0, 1),
        y_halo,
        x_halo,
    )
    total = nv * nz * rows * gy
    if gx == 4 and gy == 2 * gx and width % (2 * LANES) == 0:
        gram = gram_blocks(change, total)
    else:
        mine = jnp.moveaxis(change, 0, 1).reshape(nv * nz * rows, width)
        block_rows = lax.dot_general(
            mine,
            lax.all_gather(mine, "gx", axis=1, tiled=True),
            (((0,), (0,)), ((), ())),
            preferred_element_type=jnp.float32,
            precision=lax.Precision.HIGHEST,
        )
        gram = lax.psum_scatter(block_rows, "gy", scatter_dimension=1, tiled=True) / jnp.float32(total)
    return (by_plane(new_state), by_plane(new_register), gram)


def solution(mesh):
    tiles = P(None, None, "gy", "gx")
    in_specs = (tiles, tiles, tiles, tiles, P(None, "gy", "gx"))
    out_specs = (tiles, tiles, P("gx", "gy"))
    return jax.shard_map(on_device, mesh=mesh, in_specs=in_specs, out_specs=out_specs, check_vma=False)
```

```python
import functools

import jax
import jax.numpy as jnp
from jax import lax
from jax.experimental import pallas as pl
from jax.experimental.pallas import tpu as pltpu
from jax.sharding import PartitionSpec as P

step_size = 0.3
carry_weight = -5.0 / 9.0
update_weight = 15.0 / 16.0
LANES = 128
MESH = pl.DeviceIdType.MESH
VMEM = pltpu.VMEM
LIMIT = 56 * 2**20


def pack_columns(state, v, x_send):
    _, rows, nz, width = state.shape
    lane = lax.broadcasted_iota(jnp.int32, (nz, LANES), 1) // 2
    low = jnp.zeros((nz, LANES), jnp.float32)
    high = low
    for y in range(rows):
        first = state[v, y, :, 0:LANES]
        last = pltpu.roll(state[v, y, :, width - LANES : width], (2 * y + 2) % LANES, 1)
        low = jnp.where(lane == y, pltpu.roll(first, 2 * y, 1) if y else first, low)
        high = jnp.where(lane == y, last, high)
    x_send[0, v] = low
    x_send[1, v] = high


def beside_columns(from_right, from_left, y):
    lane = lax.broadcasted_iota(jnp.int32, from_right.shape, 1)
    right = pltpu.roll(from_right, LANES - 2 * y, 1) if y else from_right
    left = pltpu.roll(from_left, (2 * LANES - 2 - 2 * y) % LANES, 1)
    return jnp.where(lane < 2, right, left)


def halo_copies(gx, gy, state, y_halo, x_send, x_halo, y_ssem, y_rsem, x_ssem, x_rsem):
    rows = state.shape[1]
    me_x, me_y = lax.axis_index("gx"), lax.axis_index("gy")
    x_up, x_down = lax.rem(me_x + 1, gx), lax.rem(me_x + gx - 1, gx)
    y_up, y_down = lax.rem(me_y + 1, gy), lax.rem(me_y + gy - 1, gy)
    along_x, along_y = [], []
    for side, target, at in ((0, y_down, 0), (1, y_up, rows - 2)):
        along_y.append(
            pltpu.make_async_remote_copy(
                src_ref=state.at[:, at : at + 2],
                dst_ref=y_halo.at[side],
                send_sem=y_ssem.at[side],
                recv_sem=y_rsem.at[side],
                device_id=(me_x, target),
                device_id_type=MESH,
            )
        )
    for side, target in ((0, x_down), (1, x_up)):
        along_x.append(
            pltpu.make_async_remote_copy(
                src_ref=x_send.at[side],
                dst_ref=x_halo.at[side],
                send_sem=x_ssem.at[side],
                recv_sem=x_rsem.at[side],
                device_id=(target, me_y),
                device_id_type=MESH,
            )
        )
    return along_x, along_y, ((x_up, me_y), (x_down, me_y), (me_x, y_up), (me_x, y_down))


def halo_kernel(gx, gy, state, y_halo, x_halo, x_send, y_ssem, y_rsem, x_ssem, x_rsem):
    along_x, along_y, near = halo_copies(gx, gy, state, y_halo, x_send, x_halo, y_ssem, y_rsem, x_ssem, x_rsem)
    barrier = pltpu.get_barrier_semaphore()
    for device in near:
        pl.semaphore_signal(barrier, inc=1, device_id=device, device_id_type=MESH)
    for v in range(state.shape[0]):
        pack_columns(state, v, x_send)
    pl.semaphore_wait(barrier, 4)
    for copy in along_x + along_y:
        copy.start()
    for copy in along_x + along_y:
        copy.wait()


def halos(state, gx, gy):
    nv, _, nz, width = state.shape
    y_shape, x_shape = (2, nv, 2, nz, width), (2, nv, nz, LANES)
    return pl.pallas_call(
        functools.partial(halo_kernel, gx, gy),
        out_shape=(jax.ShapeDtypeStruct(y_shape, jnp.float32), jax.ShapeDtypeStruct(x_shape, jnp.float32)),
        in_specs=[pl.BlockSpec(memory_space=VMEM)],
        out_specs=[pl.BlockSpec(memory_space=VMEM)] * 2,
        scratch_shapes=[VMEM(x_shape, jnp.float32)] + [pltpu.SemaphoreType.DMA((2,))] * 4,
        compiler_params=pltpu.CompilerParams(collective_id=0, has_side_effects=True, vmem_limit_bytes=LIMIT),
    )(state)


def advance(center, beside, around, register, checkpoint, speeds, spreading):
    nz, width = center.shape
    whole = width + LANES
    wide = jnp.concatenate([center, beside], axis=1)
    along_x = [pltpu.roll(wide, k, 1)[:, :width] for k in (whole - 1, 1, whole - 2, 2)]
    along_z = [pltpu.roll(center, k, 0) for k in (nz - 1, 1, nz - 2, 2)]
    advect = near = far = None
    for speed, (p1, m1, p2, m2) in zip(speeds, (along_x, around, along_z)):
        term = speed * (8.0 * (p1 - m1) - (p2 - m2))
        advect = term if advect is None else advect + term
        near = p1 + m1 if near is None else near + (p1 + m1)
        far = p2 + m2 if far is None else far + (p2 + m2)
    spread = 16.0 * near - far - 90.0 * center
    tendency = (spreading * spread - advect) * (1.0 / 12.0)
    increment = carry_weight * register + step_size * tendency
    updated = center + update_weight * increment
    return updated, increment, updated - checkpoint.astype(jnp.float32)


def stencil_kernel(state, register, checkpoint, velocity, diffusivity, y_halo, x_halo, new_state, new_register, change):
    _, rows, nz, width = state.shape

    def plane(y):
        if y < 0:
            return y_halo[1, 0, y + 2]
        return y_halo[0, 0, y - rows] if y >= rows else state[0, y]

    for y in range(rows):
        updated, increment, moved = advance(
            plane(y),
            beside_columns(x_halo[0, 0], x_halo[1, 0], y),
            [plane(y + k) for k in (1, -1, 2, -2)],
            register[0, y],
            checkpoint[0, y],
            [velocity[d, y] for d in range(3)],
            diffusivity[y],
        )
        new_register[0, y] = increment
        new_state[0, y] = updated
        for q in range(width // LANES):
            change[q, nz * y : nz * y + nz, :] = moved[:, q * LANES : (q + 1) * LANES]


def stencil(state, register, checkpoint, velocity, diffusivity, y_halo, x_halo):
    nv, rows, nz, width = state.shape
    cells = nv * rows * nz * width
    field = pl.BlockSpec((1, rows, nz, width), lambda v: (v, 0, 0, 0))
    return pl.pallas_call(
        stencil_kernel,
        grid=(nv,),
        out_shape=(
            jax.ShapeDtypeStruct(state.shape, jnp.float32),
            jax.ShapeDtypeStruct(state.shape, jnp.float32),
            jax.ShapeDtypeStruct((width // LANES, nv * rows * nz, LANES), jnp.float32),
        ),
        in_specs=[
            field,
            field,
            field,
            pl.BlockSpec((3, rows, nz, width), lambda v: (0, 0, 0, 0)),
            pl.BlockSpec((rows, nz, width), lambda v: (0, 0, 0)),
            pl.BlockSpec((2, 1, 2, nz, width), lambda v: (0, v, 0, 0, 0)),
            pl.BlockSpec((2, 1, nz, LANES), lambda v: (0, v, 0, 0)),
        ],
        out_specs=[field, field, pl.BlockSpec((width // LANES, rows * nz, LANES), lambda v: (0, v, 0))],
        compiler_params=pltpu.CompilerParams(vmem_limit_bytes=LIMIT),
        cost_estimate=pl.CostEstimate(flops=50 * cells, bytes_accessed=28 * cells, transcendentals=0),
    )(state, register, checkpoint, velocity, diffusivity, y_halo, x_halo)


def split(value):
    high = value.astype(jnp.bfloat16)
    return high, (value - high.astype(jnp.float32)).astype(jnp.bfloat16)


def section_kernel(
    gx, gy, total, state_in, register_in, checkpoint_in, velocity_in, diffusivity_in, state_out, register_out, out,
    state, register, checkpoint, velocity, diffusivity, updated, y_halo, x_send, x_halo,
    own, held, lhs_high, lhs_low, product, y_out, y_in, kept, z_in,
    load_sem, store_sem, hy_ssem, hy_rsem, hx_ssem, hx_rsem,
    core_ssem, core_rsem, x_ssem, x_rsem, pass_ssem, pass_rsem, y_ssem, y_rsem, z_ssem, z_rsem,
):
    nv, rows, nz, width = state.shape
    chunks = width // LANES
    parts = chunks // 2
    inner = (rows - 4) * nz
    bounds = (0, (nv // 2) * inner, nv * inner, nv * rows * nz)
    i, j = lax.axis_index("gx"), lax.axis_index("gy")
    i0, i1 = lax.rem(i, 2), i // 2
    y, z = lax.rem(j, 2), j // 2
    core = (2 * i1 + 1 - i0, j)
    across = (2 * (1 - i1) + i0, j)
    y_partner = (i, 2 * z + 1 - y)
    blocks = [2 * lax.rem(i1 + s // 2, 2) + lax.rem(i0 + s % 2, 2) for s in range(4)]
    along_x, along_y, near_by = halo_copies(gx, gy, state, y_halo, x_send, x_halo, hy_ssem, hy_rsem, hx_ssem, hx_rsem)
    pairs = (
        (state_in, state),
        (velocity_in, velocity),
        (diffusivity_in, diffusivity),
        (register_in, register),
        (checkpoint_in, checkpoint),
    )
    loads = [pltpu.make_async_copy(src, dst, load_sem.at[n]) for n, (src, dst) in enumerate(pairs)]
    for load in loads:
        load.start()
    greeted = (*near_by, core, across, y_partner, *((i, 2 * lax.rem(z + k, 4) + y) for k in (1, 2, 3)))
    barrier = pltpu.get_barrier_semaphore()
    for device in greeted:
        pl.semaphore_signal(barrier, inc=1, device_id=device, device_id_type=MESH)
    loads[0].wait()
    pl.semaphore_wait(barrier, len(greeted))
    for copy in along_y:
        copy.start()

    def pack(v, _):
        pack_columns(state, v, x_send)
        return 0

    lax.fori_loop(0, nv, pack, 0)
    for copy in along_x:
        copy.start()

    def remote(src, dst, send, recv, device):
        return pltpu.make_async_remote_copy(
            src_ref=src, dst_ref=dst, send_sem=send, recv_sem=recv, device_id=device, device_id_type=MESH
        )

    def chunk_of(t):
        return lax.rem(t // parts + 1 + y, 2) * parts + lax.rem(t, parts)

    def span(k):
        return pl.ds(bounds[k], bounds[k + 1] - bounds[k])

    def x_copy(k, t):
        q = chunk_of(t)
        return remote(own.at[q, span(k)], held.at[1, q, span(k)], x_ssem.at[k, t], x_rsem.at[k, t], across)

    def pass_copy(k, t):
        q = chunk_of(t)
        return remote(held.at[1, q, span(k)], held.at[2, q, span(k)], pass_ssem.at[k, t], pass_rsem.at[k, t], core)

    def core_copy(k):
        return remote(own.at[:, span(k)], held.at[0, :, span(k)], core_ssem.at[k], core_rsem.at[k], core)

    def y_copy(s, part):
        return remote(y_out.at[s, part], y_in.at[s, part], y_ssem.at[s, part], y_rsem.at[s, part], y_partner)

    def z_copy(s, part):
        back = lax.rem(z - blocks[s] + 4, 4)
        slot = jnp.maximum(back, 1) - 1
        return remote(
            kept.at[s, part], z_in.at[slot, part], z_ssem.at[s, part], z_rsem.at[slot, part], (i, 2 * blocks[s] + y)
        )

    def compute(v, which, base):
        def plane(at):
            if at < 0:
                return y_halo[1, v, at + 2]
            return y_halo[0, v, at - rows] if at >= rows else state[v, at]

        for n, at in enumerate(which):
            fresh, increment, moved = advance(
                plane(at),
                beside_columns(x_halo[0, v], x_halo[1, v], at),
                [plane(at + k) for k in (1, -1, 2, -2)],
                register[v, at],
                checkpoint[v, at],
                [velocity[d, at] for d in range(3)],
                diffusivity[at],
            )
            register[v, at] = increment
            updated[v, at] = fresh
            place = pl.ds(pl.multiple_of(base + n * nz, nz), nz)
            for q in range(chunks):
                own[q, place, :] = moved[:, q * LANES : (q + 1) * LANES]

    def send(k):
        for t in range(chunks):
            x_copy(k, t).start()
        core_copy(k).start()

    def turn(k):
        def one(q, _):
            high, low = split(own[q, bounds[k] : bounds[k + 1], :].T)
            place = pl.ds(pl.multiple_of(q * LANES, LANES), LANES)
            lhs_high[place, bounds[k] : bounds[k + 1]] = high
            lhs_low[place, bounds[k] : bounds[k + 1]] = low
            return 0

        lax.fori_loop(0, chunks, one, 0)

    def multiply(t, left, right, k):
        block = jnp.concatenate([left[bounds[k] : bounds[k + 1], :], right[bounds[k] : bounds[k + 1], :]], axis=1)
        high, low = split(block)
        mine_high, mine_low = lhs_high[:, bounds[k] : bounds[k + 1]], lhs_low[:, bounds[k] : bounds[k + 1]]
        dot = functools.partial(jnp.dot, preferred_element_type=jnp.float32)
        term = dot(mine_high, high) + dot(mine_high, low) + dot(mine_low, high)
        if k == 0:
            product[t] = term
        else:
            product[t] += term

    def deal(base, t):
        part = lax.rem(t, parts)

        @pl.when(t < parts)
        def _():
            for s in range(2):
                y_out[base + s, part] = product[t, :, s * LANES : (s + 1) * LANES]
                y_copy(base + s, part).start()

        @pl.when(t >= parts)
        def _():
            for s in range(2):
                kept[base + s, part] = product[t, :, s * LANES : (s + 1) * LANES]

    def forward(base, part):
        for s in (base, base + 1):
            y_copy(s, part).wait_recv()
            kept[s, part] += y_in[s, part]

            @pl.when(blocks[s] != z)
            def _():
                z_copy(s, part).start()

    for load in loads[1:]:
        load.wait()
    for copy in along_x:
        copy.wait_recv()
    for k in range(2):

        def inside(v, _):
            compute(v, range(2, rows - 2), v * inner)
            return 0

        lax.fori_loop((0, nv // 2)[k], (nv // 2, nv)[k], inside, 0)
        send(k)
    for k in range(2):
        turn(k)
    for copy in along_y:
        copy.wait_recv()

    def outside(v, _):
        compute(v, (0, 1, rows - 2, rows - 1), bounds[2] + v * 4 * nz)
        return 0

    lax.fori_loop(0, nv, outside, 0)
    send(2)
    stores = [
        pltpu.make_async_copy(updated, state_out, store_sem.at[0]),
        pltpu.make_async_copy(register, register_out, store_sem.at[1]),
    ]
    for store in stores:
        store.start()
    turn(2)
    for k in range(3):
        core_copy(k).wait_recv()

    def near(t, _):
        q = chunk_of(t)
        for k in range(3):
            multiply(t, own.at[q], held.at[0, q], k)
        deal(0, t)
        return 0

    lax.fori_loop(0, chunks, near, 0)
    for k in range(2):

        def early(t, _):
            x_copy(k, t).wait_recv()
            pass_copy(k, t).start()
            return 0

        def partial(t, _):
            q = chunk_of(t)
            pass_copy(k, t).wait_recv()
            multiply(t, held.at[1, q], held.at[2, q], k)
            return 0

        lax.fori_loop(0, chunks, early, 0)
        lax.fori_loop(0, chunks, partial, 0)
        if k == 0:
            for part in range(parts):
                forward(0, part)

    def far(t, _):
        q = chunk_of(t)
        x_copy(2, t).wait_recv()
        pass_copy(2, t).start()
        pass_copy(2, t).wait_recv()
        multiply(t, held.at[1, q], held.at[2, q], 2)
        deal(2, t)

        @pl.when(t >= parts)
        def _():
            forward(2, t - parts)

        return 0

    lax.fori_loop(0, chunks, far, 0)
    for s in range(4):

        @pl.when(blocks[s] == z)
        def _():
            for part in range(parts):
                out[:, part * LANES : (part + 1) * LANES] = kept[s, part]

    for part in range(parts):
        for slot in range(3):
            remote(kept.at[0, part], z_in.at[slot, part], z_ssem.at[0, part], z_rsem.at[slot, part], core).wait_recv()
        cols = slice(part * LANES, (part + 1) * LANES)
        out[:, cols] = (out[:, cols] + z_in[0, part] + (z_in[1, part] + z_in[2, part])) / jnp.float32(total)
    for copy in along_x + along_y:
        copy.wait_send()
    for store in stores:
        store.wait()
    for k in range(3):
        core_copy(k).wait_send()
        for t in range(chunks):
            x_copy(k, t).wait_send()
            pass_copy(k, t).wait_send()
    for s in range(4):
        for part in range(parts):
            y_copy(s, part).wait_send()

            @pl.when(blocks[s] != z)
            def _():
                z_copy(s, part).wait_send()


def whole_section(arrays, gx, gy, total):
    nv, rows, nz, width = arrays[0].shape
    chunks = width // LANES
    parts = chunks // 2
    depth = nv * rows * nz
    f32 = jnp.float32
    tile = (4, parts, width, LANES)
    x_shape = (2, nv, nz, LANES)
    dma = pltpu.SemaphoreType.DMA
    whole = pl.BlockSpec(memory_space=pl.ANY)
    return pl.pallas_call(
        functools.partial(section_kernel, gx, gy, total),
        out_shape=(
            jax.ShapeDtypeStruct(arrays[0].shape, f32),
            jax.ShapeDtypeStruct(arrays[0].shape, f32),
            jax.ShapeDtypeStruct((width, parts * LANES), f32),
        ),
        in_specs=[whole] * 5,
        out_specs=(whole, whole, pl.BlockSpec(memory_space=VMEM)),
        scratch_shapes=[VMEM(array.shape, array.dtype) for array in arrays]
        + [
            VMEM(arrays[0].shape, f32),
            VMEM((2, nv, 2, nz, width), f32),
            VMEM(x_shape, f32),
            VMEM(x_shape, f32),
            VMEM((chunks, depth, LANES), f32),
            VMEM((3, chunks, depth, LANES), f32),
            VMEM((width, depth), jnp.bfloat16),
            VMEM((width, depth), jnp.bfloat16),
            VMEM((chunks, width, 2 * LANES), f32),
            VMEM(tile, f32),
            VMEM(tile, f32),
            VMEM(tile, f32),
            VMEM((3, parts, width, LANES), f32),
            dma((5,)), dma((2,)),
            dma((2,)), dma((2,)), dma((2,)), dma((2,)),
            dma((3,)), dma((3,)),
            dma((3, chunks)), dma((3, chunks)),
            dma((3, chunks)), dma((3, chunks)),
            dma((4, parts)), dma((4, parts)),
            dma((4, parts)), dma((3, parts)),
        ],
        compiler_params=pltpu.CompilerParams(collective_id=1, has_side_effects=True, vmem_limit_bytes=LIMIT),
    )(*arrays)


def on_device(state, register, checkpoint, velocity, diffusivity):
    gx, gy = lax.axis_size("gx"), lax.axis_size("gy")
    nv, nz, rows, width = state.shape
    by_plane = functools.partial(jnp.swapaxes, axis1=1, axis2=2)
    arrays = [by_plane(a) for a in (state, register, checkpoint, velocity)] + [jnp.swapaxes(diffusivity, 0, 1)]
    total = nv * nz * rows * gy
    if gx == 4 and gy == 2 * gx and width % (2 * LANES) == 0 and rows > 4:
        new_state, new_register, gram = whole_section(arrays, gx, gy, total)
    else:
        new_state, new_register, change = stencil(*arrays, *halos(arrays[0], gx, gy))
        mine = jnp.moveaxis(change, 0, 1).reshape(nv * nz * rows, width)
        block_rows = lax.dot_general(
            mine,
            lax.all_gather(mine, "gx", axis=1, tiled=True),
            (((0,), (0,)), ((), ())),
            preferred_element_type=jnp.float32,
            precision=lax.Precision.HIGHEST,
        )
        gram = lax.psum_scatter(block_rows, "gy", scatter_dimension=1, tiled=True) / jnp.float32(total)
    return (by_plane(new_state), by_plane(new_register), gram)


def solution(mesh):
    tiles = P(None, None, "gy", "gx")
    in_specs = (tiles, tiles, tiles, tiles, P(None, "gy", "gx"))
    out_specs = (tiles, tiles, P("gx", "gy"))
    return jax.shard_map(on_device, mesh=mesh, in_specs=in_specs, out_specs=out_specs, check_vma=False)
```

```python
import functools

import jax
import jax.numpy as jnp
from jax import lax
from jax.experimental import pallas as pl
from jax.experimental.pallas import tpu as pltpu
from jax.sharding import PartitionSpec as P

step_size = 0.3
carry_weight = -5.0 / 9.0
update_weight = 15.0 / 16.0
LANES = 128
MESH = pl.DeviceIdType.MESH
VMEM = pltpu.VMEM
LIMIT = 56 * 2**20


def pack_columns(state, v, x_send):
    _, rows, nz, width = state.shape
    lane = lax.broadcasted_iota(jnp.int32, (nz, LANES), 1) // 2
    low = jnp.zeros((nz, LANES), jnp.float32)
    high = low
    for y in range(rows):
        first = state[v, y, :, 0:LANES]
        last = pltpu.roll(state[v, y, :, width - LANES : width], (2 * y + 2) % LANES, 1)
        low = jnp.where(lane == y, pltpu.roll(first, 2 * y, 1) if y else first, low)
        high = jnp.where(lane == y, last, high)
    x_send[0, v] = low
    x_send[1, v] = high


def beside_columns(from_right, from_left, y):
    lane = lax.broadcasted_iota(jnp.int32, from_right.shape, 1)
    right = pltpu.roll(from_right, LANES - 2 * y, 1) if y else from_right
    left = pltpu.roll(from_left, (2 * LANES - 2 - 2 * y) % LANES, 1)
    return jnp.where(lane < 2, right, left)


def halo_copies(gx, gy, state, y_halo, x_send, x_halo, y_ssem, y_rsem, x_ssem, x_rsem):
    rows = state.shape[1]
    me_x, me_y = lax.axis_index("gx"), lax.axis_index("gy")
    x_up, x_down = lax.rem(me_x + 1, gx), lax.rem(me_x + gx - 1, gx)
    y_up, y_down = lax.rem(me_y + 1, gy), lax.rem(me_y + gy - 1, gy)
    along_x, along_y = [], []
    for side, target, at in ((0, y_down, 0), (1, y_up, rows - 2)):
        along_y.append(
            pltpu.make_async_remote_copy(
                src_ref=state.at[:, at : at + 2],
                dst_ref=y_halo.at[side],
                send_sem=y_ssem.at[side],
                recv_sem=y_rsem.at[side],
                device_id=(me_x, target),
                device_id_type=MESH,
            )
        )
    for side, target in ((0, x_down), (1, x_up)):
        along_x.append(
            pltpu.make_async_remote_copy(
                src_ref=x_send.at[side],
                dst_ref=x_halo.at[side],
                send_sem=x_ssem.at[side],
                recv_sem=x_rsem.at[side],
                device_id=(target, me_y),
                device_id_type=MESH,
            )
        )
    return along_x, along_y, ((x_up, me_y), (x_down, me_y), (me_x, y_up), (me_x, y_down))


def halo_kernel(gx, gy, state, y_halo, x_halo, x_send, y_ssem, y_rsem, x_ssem, x_rsem):
    along_x, along_y, near = halo_copies(gx, gy, state, y_halo, x_send, x_halo, y_ssem, y_rsem, x_ssem, x_rsem)
    barrier = pltpu.get_barrier_semaphore()
    for device in near:
        pl.semaphore_signal(barrier, inc=1, device_id=device, device_id_type=MESH)
    for v in range(state.shape[0]):
        pack_columns(state, v, x_send)
    pl.semaphore_wait(barrier, 4)
    for copy in along_x + along_y:
        copy.start()
    for copy in along_x + along_y:
        copy.wait()


def halos(state, gx, gy):
    nv, _, nz, width = state.shape
    y_shape, x_shape = (2, nv, 2, nz, width), (2, nv, nz, LANES)
    return pl.pallas_call(
        functools.partial(halo_kernel, gx, gy),
        out_shape=(jax.ShapeDtypeStruct(y_shape, jnp.float32), jax.ShapeDtypeStruct(x_shape, jnp.float32)),
        in_specs=[pl.BlockSpec(memory_space=VMEM)],
        out_specs=[pl.BlockSpec(memory_space=VMEM)] * 2,
        scratch_shapes=[VMEM(x_shape, jnp.float32)] + [pltpu.SemaphoreType.DMA((2,))] * 4,
        compiler_params=pltpu.CompilerParams(collective_id=0, has_side_effects=True, vmem_limit_bytes=LIMIT),
    )(state)


def advance(center, beside, around, register, checkpoint, speeds, spreading):
    nz, width = center.shape
    whole = width + LANES
    wide = jnp.concatenate([center, beside], axis=1)
    along_x = [pltpu.roll(wide, k, 1)[:, :width] for k in (whole - 1, 1, whole - 2, 2)]
    along_z = [pltpu.roll(center, k, 0) for k in (nz - 1, 1, nz - 2, 2)]
    advect = near = far = None
    for speed, (p1, m1, p2, m2) in zip(speeds, (along_x, around, along_z)):
        term = speed * (8.0 * (p1 - m1) - (p2 - m2))
        advect = term if advect is None else advect + term
        near = p1 + m1 if near is None else near + (p1 + m1)
        far = p2 + m2 if far is None else far + (p2 + m2)
    spread = 16.0 * near - far - 90.0 * center
    tendency = (spreading * spread - advect) * (1.0 / 12.0)
    increment = carry_weight * register + step_size * tendency
    updated = center + update_weight * increment
    return updated, increment, updated - checkpoint.astype(jnp.float32)


def stencil_kernel(state, register, checkpoint, velocity, diffusivity, y_halo, x_halo, new_state, new_register, change):
    _, rows, nz, width = state.shape

    def plane(y):
        if y < 0:
            return y_halo[1, 0, y + 2]
        return y_halo[0, 0, y - rows] if y >= rows else state[0, y]

    for y in range(rows):
        updated, increment, moved = advance(
            plane(y),
            beside_columns(x_halo[0, 0], x_halo[1, 0], y),
            [plane(y + k) for k in (1, -1, 2, -2)],
            register[0, y],
            checkpoint[0, y],
            [velocity[d, y] for d in range(3)],
            diffusivity[y],
        )
        new_register[0, y] = increment
        new_state[0, y] = updated
        for q in range(width // LANES):
            change[q, nz * y : nz * y + nz, :] = moved[:, q * LANES : (q + 1) * LANES]


def stencil(state, register, checkpoint, velocity, diffusivity, y_halo, x_halo):
    nv, rows, nz, width = state.shape
    cells = nv * rows * nz * width
    field = pl.BlockSpec((1, rows, nz, width), lambda v: (v, 0, 0, 0))
    return pl.pallas_call(
        stencil_kernel,
        grid=(nv,),
        out_shape=(
            jax.ShapeDtypeStruct(state.shape, jnp.float32),
            jax.ShapeDtypeStruct(state.shape, jnp.float32),
            jax.ShapeDtypeStruct((width // LANES, nv * rows * nz, LANES), jnp.float32),
        ),
        in_specs=[
            field,
            field,
            field,
            pl.BlockSpec((3, rows, nz, width), lambda v: (0, 0, 0, 0)),
            pl.BlockSpec((rows, nz, width), lambda v: (0, 0, 0)),
            pl.BlockSpec((2, 1, 2, nz, width), lambda v: (0, v, 0, 0, 0)),
            pl.BlockSpec((2, 1, nz, LANES), lambda v: (0, v, 0, 0)),
        ],
        out_specs=[field, field, pl.BlockSpec((width // LANES, rows * nz, LANES), lambda v: (0, v, 0))],
        compiler_params=pltpu.CompilerParams(vmem_limit_bytes=LIMIT),
        cost_estimate=pl.CostEstimate(flops=50 * cells, bytes_accessed=28 * cells, transcendentals=0),
    )(state, register, checkpoint, velocity, diffusivity, y_halo, x_halo)


def split(value):
    high = value.astype(jnp.bfloat16)
    return high, (value - high.astype(jnp.float32)).astype(jnp.bfloat16)


def section_kernel(
    gx, gy, total, state_in, register_in, checkpoint_in, velocity_in, diffusivity_in, state_out, register_out, out,
    state, register, checkpoint, velocity, diffusivity, updated, y_halo, x_send, x_halo,
    own, held, lhs_high, lhs_low, product, y_out, y_in, kept, z_in,
    load_sem, store_sem, hy_ssem, hy_rsem, hx_ssem, hx_rsem,
    core_ssem, core_rsem, x_ssem, x_rsem, pass_ssem, pass_rsem, y_ssem, y_rsem, z_ssem, z_rsem,
):
    nv, rows, nz, width = state.shape
    chunks = width // LANES
    parts = chunks // 2
    inner = (rows - 4) * nz
    bounds = (0, (nv // 2) * inner, nv * inner, nv * rows * nz)
    i, j = lax.axis_index("gx"), lax.axis_index("gy")
    i0, i1 = lax.rem(i, 2), i // 2
    y, z = lax.rem(j, 2), j // 2
    core = (2 * i1 + 1 - i0, j)
    across = (2 * (1 - i1) + i0, j)
    y_partner = (i, 2 * z + 1 - y)
    blocks = [2 * lax.rem(i1 + s // 2, 2) + lax.rem(i0 + s % 2, 2) for s in range(4)]
    along_x, along_y, near_by = halo_copies(gx, gy, state, y_halo, x_send, x_halo, hy_ssem, hy_rsem, hx_ssem, hx_rsem)
    pairs = (
        (state_in, state),
        (velocity_in, velocity),
        (diffusivity_in, diffusivity),
        (register_in, register),
        (checkpoint_in, checkpoint),
    )
    loads = [pltpu.make_async_copy(src, dst, load_sem.at[n]) for n, (src, dst) in enumerate(pairs)]
    for load in loads:
        load.start()
    greeted = (*near_by, core, across, y_partner, *((i, 2 * lax.rem(z + k, 4) + y) for k in (1, 2, 3)))
    barrier = pltpu.get_barrier_semaphore()
    for device in greeted:
        pl.semaphore_signal(barrier, inc=1, device_id=device, device_id_type=MESH)
    loads[0].wait()
    pl.semaphore_wait(barrier, len(greeted))
    for copy in along_y:
        copy.start()

    def pack(v, _):
        pack_columns(state, v, x_send)
        return 0

    lax.fori_loop(0, nv, pack, 0)
    for copy in along_x:
        copy.start()

    def remote(src, dst, send, recv, device):
        return pltpu.make_async_remote_copy(
            src_ref=src, dst_ref=dst, send_sem=send, recv_sem=recv, device_id=device, device_id_type=MESH
        )

    def chunk_of(t):
        return lax.rem(t + 1 + y, 2) * parts + t // 2

    def span(k):
        return pl.ds(bounds[k], bounds[k + 1] - bounds[k])

    def x_copy(k, t):
        q = chunk_of(t)
        return remote(own.at[q, span(k)], held.at[1, q, span(k)], x_ssem.at[k, t], x_rsem.at[k, t], across)

    def pass_copy(k, t):
        q = chunk_of(t)
        return remote(held.at[1, q, span(k)], held.at[2, q, span(k)], pass_ssem.at[k, t], pass_rsem.at[k, t], core)

    def core_copy(k):
        return remote(own.at[:, span(k)], held.at[0, :, span(k)], core_ssem.at[k], core_rsem.at[k], core)

    def y_copy(s, part):
        return remote(y_out.at[s, part], y_in.at[s, part], y_ssem.at[s, part], y_rsem.at[s, part], y_partner)

    def z_copy(s, part):
        back = lax.rem(z - blocks[s] + 4, 4)
        slot = jnp.maximum(back, 1) - 1
        return remote(
            kept.at[s, part], z_in.at[slot, part], z_ssem.at[s, part], z_rsem.at[slot, part], (i, 2 * blocks[s] + y)
        )

    def compute(v, which, base):
        def plane(at):
            if at < 0:
                return y_halo[1, v, at + 2]
            return y_halo[0, v, at - rows] if at >= rows else state[v, at]

        for n, at in enumerate(which):
            fresh, increment, moved = advance(
                plane(at),
                beside_columns(x_halo[0, v], x_halo[1, v], at),
                [plane(at + k) for k in (1, -1, 2, -2)],
                register[v, at],
                checkpoint[v, at],
                [velocity[d, at] for d in range(3)],
                diffusivity[at],
            )
            register[v, at] = increment
            updated[v, at] = fresh
            place = pl.ds(pl.multiple_of(base + n * nz, nz), nz)
            for q in range(chunks):
                own[q, place, :] = moved[:, q * LANES : (q + 1) * LANES]

    def turn(k):
        def one(q, _):
            high, low = split(own[q, bounds[k] : bounds[k + 1], :].T)
            place = pl.ds(pl.multiple_of(q * LANES, LANES), LANES)
            lhs_high[place, bounds[k] : bounds[k + 1]] = high
            lhs_low[place, bounds[k] : bounds[k + 1]] = low
            return 0

        lax.fori_loop(0, chunks, one, 0)

    def multiply(t, left, right, k):
        block = jnp.concatenate([left[bounds[k] : bounds[k + 1], :], right[bounds[k] : bounds[k + 1], :]], axis=1)
        high, low = split(block)
        mine_high, mine_low = lhs_high[:, bounds[k] : bounds[k + 1]], lhs_low[:, bounds[k] : bounds[k + 1]]
        dot = functools.partial(jnp.dot, preferred_element_type=jnp.float32)
        term = dot(mine_high, high) + dot(mine_high, low) + dot(mine_low, high)
        if k == 0:
            product[t] = term
        else:
            product[t] += term

    def deal(base, t):
        part = t // 2

        @pl.when(lax.rem(t, 2) == 0)
        def _():
            for s in range(2):
                y_out[base + s, part] = product[t, :, s * LANES : (s + 1) * LANES]
                y_copy(base + s, part).start()

        @pl.when(lax.rem(t, 2) == 1)
        def _():
            for s in range(2):
                kept[base + s, part] = product[t, :, s * LANES : (s + 1) * LANES]

    def forward(base, part):
        for s in (base, base + 1):
            y_copy(s, part).wait_recv()
            kept[s, part] += y_in[s, part]

            @pl.when(blocks[s] != z)
            def _():
                z_copy(s, part).start()

    for load in loads[1:]:
        load.wait()
    for copy in along_x:
        copy.wait_recv()
    for k in range(2):

        def inside(v, _):
            compute(v, range(2, rows - 2), v * inner)
            return 0

        lax.fori_loop((0, nv // 2)[k], (nv // 2, nv)[k], inside, 0)
        for t in range(1 if k else chunks):
            x_copy(k, t).start()
        core_copy(k).start()
    for k in range(2):
        turn(k)
    for copy in along_y:
        copy.wait_recv()

    def outside(v, _):
        compute(v, (0, 1, rows - 2, rows - 1), bounds[2] + v * 4 * nz)
        return 0

    lax.fori_loop(0, nv, outside, 0)
    for t in range(chunks):
        if t:
            x_copy(1, t).start()
        x_copy(2, t).start()
    core_copy(2).start()
    stores = [
        pltpu.make_async_copy(updated, state_out, store_sem.at[0]),
        pltpu.make_async_copy(register, register_out, store_sem.at[1]),
    ]
    for store in stores:
        store.start()
    turn(2)
    for k in range(3):
        core_copy(k).wait_recv()

    def near(t, _):
        q = chunk_of(t)
        for k in range(3):
            multiply(t, own.at[q], held.at[0, q], k)
        deal(0, t)
        return 0

    lax.fori_loop(0, chunks, near, 0)
    def early(t, _):
        x_copy(0, t).wait_recv()
        pass_copy(0, t).start()
        return 0

    def partial(t, _):
        q = chunk_of(t)
        pass_copy(0, t).wait_recv()
        multiply(t, held.at[1, q], held.at[2, q], 0)
        return 0

    lax.fori_loop(0, chunks, early, 0)
    lax.fori_loop(0, chunks, partial, 0)

    def far(t, _):
        q = chunk_of(t)
        for k in (1, 2):
            x_copy(k, t).wait_recv()
            pass_copy(k, t).start()
        for k in (1, 2):
            pass_copy(k, t).wait_recv()
            multiply(t, held.at[1, q], held.at[2, q], k)
        deal(2, t)

        @pl.when(lax.rem(t, 2) == 0)
        def _():
            forward(0, t // 2)

        @pl.when(lax.rem(t, 2) == 1)
        def _():
            forward(2, t // 2)

        return 0

    lax.fori_loop(0, chunks, far, 0)
    for s in range(4):

        @pl.when(blocks[s] == z)
        def _():
            for part in range(parts):
                out[:, part * LANES : (part + 1) * LANES] = kept[s, part]

    for part in range(parts):
        for slot in range(3):
            remote(kept.at[0, part], z_in.at[slot, part], z_ssem.at[0, part], z_rsem.at[slot, part], core).wait_recv()
        cols = slice(part * LANES, (part + 1) * LANES)
        out[:, cols] = (out[:, cols] + z_in[0, part] + (z_in[1, part] + z_in[2, part])) / jnp.float32(total)
    for copy in along_x + along_y:
        copy.wait_send()
    for store in stores:
        store.wait()
    for k in range(3):
        core_copy(k).wait_send()
        for t in range(chunks):
            x_copy(k, t).wait_send()
            pass_copy(k, t).wait_send()
    for s in range(4):
        for part in range(parts):
            y_copy(s, part).wait_send()

            @pl.when(blocks[s] != z)
            def _():
                z_copy(s, part).wait_send()


def whole_section(arrays, gx, gy, total):
    nv, rows, nz, width = arrays[0].shape
    chunks = width // LANES
    parts = chunks // 2
    depth = nv * rows * nz
    f32 = jnp.float32
    tile = (4, parts, width, LANES)
    x_shape = (2, nv, nz, LANES)
    dma = pltpu.SemaphoreType.DMA
    whole = pl.BlockSpec(memory_space=pl.ANY)
    return pl.pallas_call(
        functools.partial(section_kernel, gx, gy, total),
        out_shape=(
            jax.ShapeDtypeStruct(arrays[0].shape, f32),
            jax.ShapeDtypeStruct(arrays[0].shape, f32),
            jax.ShapeDtypeStruct((width, parts * LANES), f32),
        ),
        in_specs=[whole] * 5,
        out_specs=(whole, whole, pl.BlockSpec(memory_space=VMEM)),
        scratch_shapes=[VMEM(array.shape, array.dtype) for array in arrays]
        + [
            VMEM(arrays[0].shape, f32),
            VMEM((2, nv, 2, nz, width), f32),
            VMEM(x_shape, f32),
            VMEM(x_shape, f32),
            VMEM((chunks, depth, LANES), f32),
            VMEM((3, chunks, depth, LANES), f32),
            VMEM((width, depth), jnp.bfloat16),
            VMEM((width, depth), jnp.bfloat16),
            VMEM((chunks, width, 2 * LANES), f32),
            VMEM(tile, f32),
            VMEM(tile, f32),
            VMEM(tile, f32),
            VMEM((3, parts, width, LANES), f32),
            dma((5,)), dma((2,)),
            dma((2,)), dma((2,)), dma((2,)), dma((2,)),
            dma((3,)), dma((3,)),
            dma((3, chunks)), dma((3, chunks)),
            dma((3, chunks)), dma((3, chunks)),
            dma((4, parts)), dma((4, parts)),
            dma((4, parts)), dma((3, parts)),
        ],
        compiler_params=pltpu.CompilerParams(collective_id=1, has_side_effects=True, vmem_limit_bytes=LIMIT),
    )(*arrays)


def on_device(state, register, checkpoint, velocity, diffusivity):
    gx, gy = lax.axis_size("gx"), lax.axis_size("gy")
    nv, nz, rows, width = state.shape
    by_plane = functools.partial(jnp.swapaxes, axis1=1, axis2=2)
    arrays = [by_plane(a) for a in (state, register, checkpoint, velocity)] + [jnp.swapaxes(diffusivity, 0, 1)]
    total = nv * nz * rows * gy
    if gx == 4 and gy == 2 * gx and width % (2 * LANES) == 0 and rows > 4:
        new_state, new_register, gram = whole_section(arrays, gx, gy, total)
    else:
        new_state, new_register, change = stencil(*arrays, *halos(arrays[0], gx, gy))
        mine = jnp.moveaxis(change, 0, 1).reshape(nv * nz * rows, width)
        block_rows = lax.dot_general(
            mine,
            lax.all_gather(mine, "gx", axis=1, tiled=True),
            (((0,), (0,)), ((), ())),
            preferred_element_type=jnp.float32,
            precision=lax.Precision.HIGHEST,
        )
        gram = lax.psum_scatter(block_rows, "gy", scatter_dimension=1, tiled=True) / jnp.float32(total)
    return (by_plane(new_state), by_plane(new_register), gram)


def solution(mesh):
    tiles = P(None, None, "gy", "gx")
    in_specs = (tiles, tiles, tiles, tiles, P(None, "gy", "gx"))
    out_specs = (tiles, tiles, P("gx", "gy"))
    return jax.shard_map(on_device, mesh=mesh, in_specs=in_specs, out_specs=out_specs, check_vma=False)
```
